32 devices in a mesh: seq: 16 (over z, y, x), kmer: 2 (over core).
Axes of the slice: x: 2, y: 2, z: 4, core: 2. Of those that a mesh axis runs over, the one named last changes fastest.
Arguments:
- profiles: bfloat16 [2048, 16384], P(('seq', 'kmer')), may hold values from -6 to 6
- lengths: int32 [16384], P('seq'), may hold values from 64 to 1024
- owners: int32 [2], replicated, may hold values from 0 to 15
- block_mask: int32 [2, 128, 8], P(None, 'seq'), may hold values 0 or 1
Outputs:
- scores: bfloat16 [16384, 2, 1024], P('seq', None, 'kmer')
The draws below stay inside these ranges and needn't reach their ends.
All inputs are finite; a program needn't handle non-finite values. No bound on the sum of `block_mask` on one device may be relied on, other than what follows from the above.
Results may differ from the reference program's by a relative error of at most 0.001.
Values may be sent and summed in bfloat16 or wider, within the bound.
A program may use at most 64 MiB of HBM per device.

```python
import jax
import jax.numpy as jnp
from jax import lax

KM = 2048
PANEL = 1024
BLK = 128
SECTIONS = 2
NSEQ = 16384
N_SEQ = 16


def touch_ends(values, own_key, low, top_value):
    longest = values.shape.index(max(values.shape))
    spots = []
    for shift in (0, 1):
        where = [jax.random.randint(jax.random.fold_in(own_key, axis), (), 0, length) for axis, length in enumerate(values.shape)]
        where[longest] = (where[longest] + shift) % values.shape[longest]
        spots.append(tuple(where))
    return values.at[spots[0]].set(low).at[spots[1]].set(top_value)


def block_levels(key, shape, split, least, top_value):
    def one(position, parts):
        steps = jax.random.uniform(jax.random.fold_in(jax.random.fold_in(key, 6), position), (parts,), jnp.float32, least / len(split), top_value / len(split))
        return jnp.repeat(jnp.exp(steps), shape[position] // parts).reshape((-1,) + (1,) * (len(shape) - position - 1))

    gain = one(*split[0])
    for cut in split[1:]:
        gain = gain * one(*cut)
    return gain


def noise(rng, shape, scale, reach, split=(), held_as=jnp.bfloat16):
    result = scale * jax.random.normal(rng, shape, jnp.float32)
    if split:
        result = result * block_levels(rng, shape, split, -0.22, 0.18)
    return jnp.clip(result, -reach, reach).astype(held_as)


def setup_inputs(seed: int = 0) -> dict:
    splits = jax.random.split(jax.random.key(seed), 5)
    profiles = noise(splits[0], (KM, NSEQ), 1.0, 6.0, ((0, 32),))
    lengths = touch_ends(jax.random.randint(splits[1], (NSEQ,), 64, 1025), jax.random.fold_in(splits[1], 1), 64, 1024).astype(jnp.int32)
    owners = jax.random.randint(splits[2], (SECTIONS,), 0, N_SEQ).astype(jnp.int32)
    block_mask = touch_ends((jax.random.randint(splits[3], (SECTIONS, NSEQ // BLK, PANEL // BLK), 0, 5) < 2).astype(jnp.int32), jax.random.fold_in(splits[3], 1), 0, 1)
    return {"profiles": profiles, "lengths": lengths, "owners": owners, "block_mask": block_mask}


def reference(profiles, lengths, owners, block_mask):
    prof = profiles.astype(jnp.float32)
    row_len = lengths.astype(jnp.float32)
    scale = 256.0 / jnp.sqrt(jnp.float32(KM))
    outs = []
    for section in range(SECTIONS):
        start = owners[section].astype(jnp.int32) * PANEL
        panel = lax.dynamic_slice_in_dim(prof, start, PANEL, 1)
        col_len = lax.dynamic_slice_in_dim(row_len, start, PANEL, 0)
        raw = jnp.dot(prof.T, panel, preferred_element_type=jnp.float32)
        mask = jnp.repeat(jnp.repeat(block_mask[section], BLK, axis=0), BLK, axis=1).astype(jnp.float32)
        norm = scale * lax.rsqrt(row_len[:, None] * col_len[None, :])
        outs.append((raw * norm * mask).astype(jnp.bfloat16))
    return jnp.stack(outs, axis=1)
```

```python
import functools

import jax
import jax.numpy as jnp
from jax import lax
from jax.experimental import pallas as pl
from jax.experimental.pallas import tpu as pltpu
from jax.sharding import PartitionSpec as P

KM = 2048
BLK = 128
SECTIONS = 2
MESH = pl.DeviceIdType.MESH


def broadcast(block, axis, source):
    block = jnp.where(lax.axis_index(axis) == source, block, jnp.zeros_like(block))
    return lax.psum(block, axis)


def shards(profiles, lengths, owners, block_mask):
    local = lax.all_to_all(profiles, "seq", split_axis=1, concat_axis=0, tiled=True)
    panel_rows = local.shape[1]
    half = panel_rows // 2
    part = lax.axis_index("kmer")
    row_len = lengths.astype(jnp.float32)
    scale = 256.0 / jnp.sqrt(jnp.float32(KM))
    contract = (((0,), (0,)), ((), ()))
    outs = []
    for section in range(SECTIONS):
        panel, panel_len = (
            broadcast(local, "seq", owners[section]),
            broadcast(lengths, "seq", owners[section]),
        )
        partial_value = lax.dot_general(local, panel, contract, preferred_element_type=jnp.float32)
        raw = lax.psum_scatter(partial_value, "kmer", scatter_dimension=1, tiled=True)
        col_len = lax.dynamic_slice_in_dim(panel_len.astype(jnp.float32), part * half, half, 0)
        mask_full = jnp.repeat(jnp.repeat(block_mask[section], BLK, axis=0), BLK, axis=1).astype(
            jnp.float32
        )
        mask = lax.dynamic_slice_in_dim(mask_full, part * half, half, 1)
        norm = scale * lax.rsqrt(row_len[:, None] * col_len[None, :])
        outs.append((raw * norm * mask).astype(jnp.bfloat16))
    return jnp.stack(outs, axis=1)


PLANES, ACROSS = 4, 4


def kernel(
    prof_hbm, mine_hbm, lens_hbm, owners, mask, out, prof, panel, local, acc, lens, lens_all,
    in_sem, ex_sem, p_send, p_recv, l_send, l_recv, f_send, len_send, len_recv,
):
    n = PLANES * ACROSS
    feats = prof.shape[0]
    size = local.shape[1]
    half = size // 2
    me, core = lax.axis_index("seq"), lax.axis_index("kmer")
    sib = 1 - core
    z, xy = lax.div(me, ACROSS), lax.rem(me, ACROSS)
    y, x = lax.div(xy, 2), lax.rem(xy, 2)
    xn = me + 1 - 2 * x
    yn = me + 2 * (1 - 2 * y)
    high = lax.div(z, 2)
    order = [z, z + 1 - 2 * lax.rem(z, 2), 2 - high, 3 - 3 * high]
    shift = [(p - z) * ACROSS for p in order]
    inner = jnp.logical_or(z == 1, z == 2)
    pair, middle = me + shift[1], me + ACROSS * (3 - 2 * z)

    def rows(place, c):
        return pl.ds(pl.multiple_of((place * 2 + c) * feats, feats), feats)

    def columns(start, length):
        return pl.ds(pl.multiple_of(start, length), length)

    def piece(place, c, slot, to):
        at = panel.at[rows(place, c)]
        i = place * 2 + c
        return pltpu.make_async_remote_copy(
            src_ref=at, dst_ref=at, send_sem=p_send.at[i * 4 + slot], recv_sem=p_recv.at[i],
            device_id=(to, core), device_id_type=MESH,
        )

    def block_to(to):
        return pltpu.make_async_remote_copy(
            src_ref=prof.at[:, columns(to * size, size)], dst_ref=local.at[rows(me, core)],
            send_sem=l_send.at[to], recv_sem=l_recv.at[me * 2 + core],
            device_id=(to, core), device_id_type=MESH,
        )

    def lens_to(to):
        return pltpu.make_async_remote_copy(
            src_ref=lens.at[core], dst_ref=lens_all.at[me],
            send_sem=len_send.at[to], recv_sem=len_recv.at[me],
            device_id=(to, core), device_id_type=MESH,
        )

    def hand_over(place, own=False):
        at = local.at[rows(place, core)]
        return pltpu.make_async_remote_copy(
            src_ref=prof.at[:, columns(me * size, size)] if own else at, dst_ref=at,
            send_sem=f_send.at[place], recv_sem=l_recv.at[place * 2 + core],
            device_id=(me, sib), device_id_type=MESH,
        )

    def local_arrived(place, c):
        at = local.at[rows(place, c)]
        pltpu.make_async_remote_copy(
            src_ref=at, dst_ref=at, send_sem=f_send.at[place], recv_sem=l_recv.at[place * 2 + c],
            device_id=(me, sib), device_id_type=MESH,
        ).wait_recv()

    load = pltpu.make_async_copy(prof_hbm, prof, in_sem.at[0])
    load.start()
    load_lens = pltpu.make_async_copy(lens_hbm, lens, in_sem.at[1])
    load_lens.start()

    load_mine = pltpu.make_async_copy(mine_hbm.at[core], panel.at[rows(me, core)], in_sem.at[2])
    load_mine.start()

    barrier = pltpu.get_barrier_semaphore()

    @pl.loop(1, n)
    def _(i):
        pl.semaphore_signal(
            barrier, inc=1, device_id=(lax.rem(me + i, n), core), device_id_type=MESH
        )

    pl.semaphore_signal(barrier, inc=1, device_id=(me, sib), device_id_type=MESH)
    load.wait()
    load_lens.wait()
    load_mine.wait()
    local[rows(me, core), :] = prof[:, columns(me * size, size)]
    lens_all[me] = lens[core]
    pl.semaphore_wait(barrier, n)

    exchange = pltpu.make_async_remote_copy(
        src_ref=mine_hbm.at[sib], dst_ref=panel.at[rows(me, core)], send_sem=ex_sem,
        recv_sem=p_recv.at[me * 2 + core], device_id=(me, sib), device_id_type=MESH,
    )
    exchange.start()

    def spread(q, c):
        place = me + shift[q]
        if q == 0:
            piece(place, c, 0, pair).start()

            @pl.when(inner)
            def _():
                piece(place, c, 1, middle).start()
        else:
            piece(place, c, 0, pair).wait_recv()

            @pl.when(inner)
            def _():
                piece(place, c, 0, middle if q == 1 else pair).start()

        piece(place, c, 2, xn).start()
        piece(place, c, 3, yn).start()

    def cross(q):
        piece(xn + shift[q], 0, 3, yn).wait_recv()
        piece(xn + shift[q], 0, 3, yn).start()
        piece(yn + shift[q], 1, 2, xn).wait_recv()
        piece(yn + shift[q], 1, 2, xn).start()

    def pass_on(q):
        for j in range(ACROSS):
            if q == 0 and j == 0:
                continue
            place = order[q] * ACROSS + lax.rem(xy + j, ACROSS)
            local_arrived(place, core)
            hand_over(place).start()

    def multiply(q):
        for j in range(ACROSS):
            local_arrived(order[q] * ACROSS + lax.rem(xy + j, ACROSS), sib)
        piece(xn + shift[q], 1, 3, yn).wait_recv()
        piece(yn + shift[q], 0, 3, yn).wait_recv()
        diagonal = xn + yn - me + shift[q]
        for c in range(2):
            piece(diagonal, c, 0, yn).wait_recv()
        deep = ACROSS * 2 * feats
        span = pl.ds(pl.multiple_of(order[q] * deep, deep), deep)

        @pl.loop(0, size // 256)
        def _(i):
            at = pl.ds(pl.multiple_of(i * 256, 256), 256)
            value = lax.dot_general(
                local[span, at], panel[span, :], (((0,), (0,)), ((), ())),
                preferred_element_type=jnp.float32,
            )
            if q == 0:
                acc[at, :] = value
            else:
                acc[at, :] += value

    place = me
    piece(place, core, 0, pair).start()

    @pl.when(inner)
    def _():
        piece(place, core, 1, middle).start()

    piece(place, core, 2, xn).start()
    piece(place, core, 3, yn).start()
    hand_over(me, own=True).start()
    piece(place, sib, 0, pair).wait_recv()
    spread(0, sib)

    for j in range(ACROSS):
        for q in (2, 3, 1, 0):
            if q == 0 and j == 0:
                continue
            to = order[q] * ACROSS + lax.rem(xy + j, ACROSS)
            block_to(to).start()
            lens_to(to).start()

    for q in range(1, PLANES):
        spread(q, 0)
        spread(q, 1)
        cross(q - 1)
        if q >= 2:
            pass_on(q - 2)
        if q >= 3:
            multiply(q - 3)
    cross(3)
    pass_on(2)
    multiply(1)
    pass_on(3)
    multiply(2)

    @pl.loop(1, n)
    def _(i):
        other = lax.rem(me + i, n)
        pltpu.make_async_remote_copy(
            src_ref=lens.at[core], dst_ref=lens_all.at[other],
            send_sem=len_send.at[other], recv_sem=len_recv.at[other],
            device_id=(other, core), device_id_type=MESH,
        ).wait_recv()

    multiply(3)

    scale = 256.0 / jnp.sqrt(jnp.float32(KM))
    for t in range(SECTIONS):
        col_len = jnp.zeros(lens_all.shape[1:], jnp.int32)
        for i in range(n):
            off = owners[t] - i
            col_len += jnp.maximum(1 - off * off, 0) * lens_all[i]
        col_len = col_len.astype(jnp.float32)

        @pl.loop(0, 2)
        def _(h):
            for r in range(size // BLK // 2):
                i = h * (size // BLK // 2) + r
                row = lens[h, r:r + 1, :].astype(jnp.float32)
                row_len = jnp.broadcast_to(row, (BLK, BLK)).T
                at = pl.ds(pl.multiple_of(i * BLK, BLK), BLK)
                for j in range(half // BLK):
                    spot = slice(j * BLK, (j + 1) * BLK)
                    norm = scale * lax.rsqrt(row_len * col_len[j:j + 1, :])
                    scored = mask[t, i, core * (half // BLK) + j].astype(jnp.float32)
                    raw = acc[at, t * half + j * BLK:t * half + (j + 1) * BLK]
                    out[t, at, spot] = (raw * norm * scored).astype(out.dtype)

    exchange.wait_send()
    for c in range(2):
        piece(me, c, 0, pair).wait_send()
        piece(me, c, 2, xn).wait_send()
        piece(me, c, 3, yn).wait_send()
        for q in range(1, PLANES):
            piece(me + shift[q], c, 2, xn).wait_send()
            piece(me + shift[q], c, 3, yn).wait_send()

    @pl.when(inner)
    def _():
        for c in range(2):
            piece(me, c, 1, middle).wait_send()
            for q in range(1, PLANES):
                piece(me + shift[q], c, 0, pair).wait_send()

    for q in range(PLANES):
        piece(xn + shift[q], 0, 3, yn).wait_send()
        piece(yn + shift[q], 1, 2, xn).wait_send()
    hand_over(me, own=True).wait_send()

    @pl.loop(1, n)
    def _(i):
        other = lax.rem(me + i, n)
        block_to(other).wait_send()
        lens_to(other).wait_send()
        hand_over(other).wait_send()


def fused(profiles, lengths, owners, block_mask):
    n = PLANES * ACROSS
    feats, size = profiles.shape[0], lengths.shape[0]
    half = size // 2
    lens = lengths.reshape(2, half // BLK, BLK)
    parts = [
        lax.dynamic_slice_in_dim(profiles, owners[t] * size, size, 1).reshape(feats, 2, half)
        for t in range(SECTIONS)
    ]
    mine = jnp.concatenate(parts, axis=2).transpose(1, 0, 2)
    out = pl.pallas_call(
        kernel,
        out_shape=jax.ShapeDtypeStruct((SECTIONS, size, half), jnp.bfloat16),
        in_specs=[
            pl.BlockSpec(memory_space=pl.ANY),
            pl.BlockSpec(memory_space=pl.ANY),
            pl.BlockSpec(memory_space=pl.ANY),
            pl.BlockSpec(memory_space=pltpu.SMEM),
            pl.BlockSpec(memory_space=pltpu.SMEM),
        ],
        out_specs=pl.BlockSpec(memory_space=pltpu.VMEM),
        scratch_shapes=[
            pltpu.VMEM(profiles.shape, jnp.bfloat16),
            pltpu.VMEM((KM, size), jnp.bfloat16),
            pltpu.VMEM((KM, size), jnp.bfloat16),
            pltpu.VMEM((size, size), jnp.float32),
            pltpu.VMEM(lens.shape, jnp.int32),
            pltpu.VMEM((n,) + lens.shape[1:], jnp.int32),
            pltpu.SemaphoreType.DMA((3,)),
            pltpu.SemaphoreType.DMA,
            pltpu.SemaphoreType.DMA((n * 2 * 4,)),
            pltpu.SemaphoreType.DMA((n * 2,)),
            pltpu.SemaphoreType.DMA((n,)),
            pltpu.SemaphoreType.DMA((n * 2,)),
            pltpu.SemaphoreType.DMA((n,)),
            pltpu.SemaphoreType.DMA((n,)),
            pltpu.SemaphoreType.DMA((n,)),
        ],
        compiler_params=pltpu.CompilerParams(
            collective_id=0, has_side_effects=True, vmem_limit_bytes=48 * 1024 * 1024
        ),
        cost_estimate=pl.CostEstimate(
            flops=2 * KM * size * size, bytes_accessed=8 * 1024 * 1024, transcendentals=size * size
        ),
    )(profiles, mine, lens, owners, block_mask)
    return out.transpose(1, 0, 2)


def solution(mesh):
    placed = (P(("seq", "kmer"), None), P("seq"), P(), P(None, "seq", None))
    n, cores = mesh.shape["seq"], mesh.shape["kmer"]
    fits = n == PLANES * ACROSS and cores == 2
    return jax.shard_map(
        fused if fits else shards,
        mesh=mesh, in_specs=placed, out_specs=P("seq", None, "kmer"), check_vma=False,
    )
```

```python
import functools

import jax
import jax.numpy as jnp
from jax import lax
from jax.experimental import pallas as pl
from jax.experimental.pallas import tpu as pltpu
from jax.sharding import PartitionSpec as P

KM = 2048
BLK = 128
SECTIONS = 2
MESH = pl.DeviceIdType.MESH


def broadcast(block, axis, source):
    block = jnp.where(lax.axis_index(axis) == source, block, jnp.zeros_like(block))
    return lax.psum(block, axis)


def shards(profiles, lengths, owners, block_mask):
    local = lax.all_to_all(profiles, "seq", split_axis=1, concat_axis=0, tiled=True)
    panel_rows = local.shape[1]
    half = panel_rows // 2
    part = lax.axis_index("kmer")
    row_len = lengths.astype(jnp.float32)
    scale = 256.0 / jnp.sqrt(jnp.float32(KM))
    contract = (((0,), (0,)), ((), ()))
    outs = []
    for section in range(SECTIONS):
        panel, panel_len = (
            broadcast(local, "seq", owners[section]),
            broadcast(lengths, "seq", owners[section]),
        )
        partial_value = lax.dot_general(local, panel, contract, preferred_element_type=jnp.float32)
        raw = lax.psum_scatter(partial_value, "kmer", scatter_dimension=1, tiled=True)
        col_len = lax.dynamic_slice_in_dim(panel_len.astype(jnp.float32), part * half, half, 0)
        mask_full = jnp.repeat(jnp.repeat(block_mask[section], BLK, axis=0), BLK, axis=1).astype(
            jnp.float32
        )
        mask = lax.dynamic_slice_in_dim(mask_full, part * half, half, 1)
        norm = scale * lax.rsqrt(row_len[:, None] * col_len[None, :])
        outs.append((raw * norm * mask).astype(jnp.bfloat16))
    return jnp.stack(outs, axis=1)


PLANES, ACROSS = 4, 4


def kernel(
    prof_hbm, first, second, lens_hbm, owners, mask, out, prof, ex, panel, local, acc, lens, lens_all,
    in_sem, ex_sem, p_send, p_recv, l_send, l_recv, f_send, len_send, len_recv,
):
    n = PLANES * ACROSS
    feats = prof.shape[0]
    size = local.shape[1]
    half = size // 2
    me, core = lax.axis_index("seq"), lax.axis_index("kmer")
    sib = 1 - core
    z, xy = lax.div(me, ACROSS), lax.rem(me, ACROSS)
    y, x = lax.div(xy, 2), lax.rem(xy, 2)
    xn = me + 1 - 2 * x
    yn = me + 2 * (1 - 2 * y)
    high = lax.div(z, 2)
    order = [z, z + 1 - 2 * lax.rem(z, 2), 2 - high, 3 - 3 * high]
    shift = [(p - z) * ACROSS for p in order]
    inner = jnp.logical_or(z == 1, z == 2)
    pair, middle = me + shift[1], me + ACROSS * (3 - 2 * z)

    def rows(place, c):
        return pl.ds(pl.multiple_of((place * 2 + c) * feats, feats), feats)

    def columns(start, length):
        return pl.ds(pl.multiple_of(start, length), length)

    def piece(place, c, slot, to):
        at = panel.at[rows(place, c)]
        i = place * 2 + c
        return pltpu.make_async_remote_copy(
            src_ref=at, dst_ref=at, send_sem=p_send.at[i * 4 + slot], recv_sem=p_recv.at[i],
            device_id=(to, core), device_id_type=MESH,
        )

    def block_to(to):
        return pltpu.make_async_remote_copy(
            src_ref=prof.at[:, columns(to * size, size)], dst_ref=local.at[rows(me, core)],
            send_sem=l_send.at[to], recv_sem=l_recv.at[me * 2 + core],
            device_id=(to, core), device_id_type=MESH,
        )

    def lens_to(to):
        return pltpu.make_async_remote_copy(
            src_ref=lens.at[core], dst_ref=lens_all.at[me],
            send_sem=len_send.at[to], recv_sem=len_recv.at[me],
            device_id=(to, core), device_id_type=MESH,
        )

    def hand_over(place, own=False):
        at = local.at[rows(place, core)]
        return pltpu.make_async_remote_copy(
            src_ref=prof.at[:, columns(me * size, size)] if own else at, dst_ref=at,
            send_sem=f_send.at[place], recv_sem=l_recv.at[place * 2 + core],
            device_id=(me, sib), device_id_type=MESH,
        )

    def local_arrived(place, c):
        at = local.at[rows(place, c)]
        pltpu.make_async_remote_copy(
            src_ref=at, dst_ref=at, send_sem=f_send.at[place], recv_sem=l_recv.at[place * 2 + c],
            device_id=(me, sib), device_id_type=MESH,
        ).wait_recv()

    load = pltpu.make_async_copy(prof_hbm, prof, in_sem.at[0])
    load.start()
    load_lens = pltpu.make_async_copy(lens_hbm, lens, in_sem.at[1])
    load_lens.start()

    own_half, other_half = columns(core * half, half), columns(sib * half, half)
    load_mine = []
    for t, part in enumerate((first, second)):
        spot = pl.ds(t * half, half)
        load_mine.append(pltpu.make_async_copy(
            part.at[:, own_half], panel.at[rows(me, core), spot], in_sem.at[2 + t]
        ))
        load_mine.append(pltpu.make_async_copy(
            part.at[:, other_half], ex.at[:, spot], in_sem.at[4 + t]
        ))
    for step in load_mine:
        step.start()

    barrier = pltpu.get_barrier_semaphore()

    @pl.loop(1, n)
    def _(i):
        pl.semaphore_signal(
            barrier, inc=1, device_id=(lax.rem(me + i, n), core), device_id_type=MESH
        )

    pl.semaphore_signal(barrier, inc=1, device_id=(me, sib), device_id_type=MESH)
    load.wait()
    load_lens.wait()
    for step in load_mine:
        step.wait()
    local[rows(me, core), :] = prof[:, columns(me * size, size)]
    lens_all[me] = lens[core]
    pl.semaphore_wait(barrier, n)

    exchange = pltpu.make_async_remote_copy(
        src_ref=ex, dst_ref=panel.at[rows(me, core)], send_sem=ex_sem,
        recv_sem=p_recv.at[me * 2 + core], device_id=(me, sib), device_id_type=MESH,
    )
    exchange.start()

    def spread(q, c):
        place = me + shift[q]
        if q == 0:
            piece(place, c, 0, pair).start()

            @pl.when(inner)
            def _():
                piece(place, c, 1, middle).start()
        else:
            piece(place, c, 0, pair).wait_recv()

            @pl.when(inner)
            def _():
                piece(place, c, 0, middle if q == 1 else pair).start()

        piece(place, c, 2, xn).start()
        piece(place, c, 3, yn).start()

    def cross(q):
        piece(xn + shift[q], 0, 3, yn).wait_recv()
        piece(xn + shift[q], 0, 3, yn).start()
        piece(yn + shift[q], 1, 2, xn).wait_recv()
        piece(yn + shift[q], 1, 2, xn).start()

    def pass_on(q):
        for j in range(ACROSS):
            if q == 0 and j == 0:
                continue
            place = order[q] * ACROSS + lax.rem(xy + j, ACROSS)
            local_arrived(place, core)
            hand_over(place).start()

    def multiply(q):
        for j in range(ACROSS):
            local_arrived(order[q] * ACROSS + lax.rem(xy + j, ACROSS), sib)
        piece(xn + shift[q], 1, 3, yn).wait_recv()
        piece(yn + shift[q], 0, 3, yn).wait_recv()
        diagonal = xn + yn - me + shift[q]
        for c in range(2):
            piece(diagonal, c, 0, yn).wait_recv()
        deep = ACROSS * 2 * feats
        span = pl.ds(pl.multiple_of(order[q] * deep, deep), deep)

        @pl.loop(0, size // 256)
        def _(i):
            at = pl.ds(pl.multiple_of(i * 256, 256), 256)
            value = lax.dot_general(
                local[span, at], panel[span, :], (((0,), (0,)), ((), ())),
                preferred_element_type=jnp.float32,
            )
            if q == 0:
                acc[at, :] = value
            else:
                acc[at, :] += value

    place = me
    piece(place, core, 0, pair).start()

    @pl.when(inner)
    def _():
        piece(place, core, 1, middle).start()

    piece(place, core, 2, xn).start()
    piece(place, core, 3, yn).start()
    hand_over(me, own=True).start()
    piece(place, sib, 0, pair).wait_recv()
    spread(0, sib)

    for j in range(ACROSS):
        for q in (2, 3, 1, 0):
            if q == 0 and j == 0:
                continue
            to = order[q] * ACROSS + lax.rem(xy + j, ACROSS)
            block_to(to).start()
            lens_to(to).start()

    for q in range(1, PLANES):
        spread(q, 0)
        spread(q, 1)
        cross(q - 1)
        if q >= 2:
            pass_on(q - 2)
        if q >= 3:
            multiply(q - 3)
    cross(3)
    pass_on(2)
    multiply(1)
    pass_on(3)
    multiply(2)

    @pl.loop(1, n)
    def _(i):
        other = lax.rem(me + i, n)
        pltpu.make_async_remote_copy(
            src_ref=lens.at[core], dst_ref=lens_all.at[other],
            send_sem=len_send.at[other], recv_sem=len_recv.at[other],
            device_id=(other, core), device_id_type=MESH,
        ).wait_recv()

    multiply(3)

    scale = 256.0 / jnp.sqrt(jnp.float32(KM))
    for t in range(SECTIONS):
        col_len = jnp.zeros(lens_all.shape[1:], jnp.int32)
        for i in range(n):
            off = owners[t] - i
            col_len += jnp.maximum(1 - off * off, 0) * lens_all[i]
        col_len = col_len.astype(jnp.float32)

        @pl.loop(0, 2)
        def _(h):
            for r in range(size // BLK // 2):
                i = h * (size // BLK // 2) + r
                row = lens[h, r:r + 1, :].astype(jnp.float32)
                row_len = jnp.broadcast_to(row, (BLK, BLK)).T
                at = pl.ds(pl.multiple_of(i * BLK, BLK), BLK)
                for j in range(half // BLK):
                    spot = slice(j * BLK, (j + 1) * BLK)
                    norm = scale * lax.rsqrt(row_len * col_len[j:j + 1, :])
                    scored = mask[t, i, core * (half // BLK) + j].astype(jnp.float32)
                    raw = acc[at, t * half + j * BLK:t * half + (j + 1) * BLK]
                    out[t, at, spot] = (raw * norm * scored).astype(out.dtype)

    exchange.wait_send()
    for c in range(2):
        piece(me, c, 0, pair).wait_send()
        piece(me, c, 2, xn).wait_send()
        piece(me, c, 3, yn).wait_send()
        for q in range(1, PLANES):
            piece(me + shift[q], c, 2, xn).wait_send()
            piece(me + shift[q], c, 3, yn).wait_send()

    @pl.when(inner)
    def _():
        for c in range(2):
            piece(me, c, 1, middle).wait_send()
            for q in range(1, PLANES):
                piece(me + shift[q], c, 0, pair).wait_send()

    for q in range(PLANES):
        piece(xn + shift[q], 0, 3, yn).wait_send()
        piece(yn + shift[q], 1, 2, xn).wait_send()
    hand_over(me, own=True).wait_send()

    @pl.loop(1, n)
    def _(i):
        other = lax.rem(me + i, n)
        block_to(other).wait_send()
        lens_to(other).wait_send()
        hand_over(other).wait_send()


def fused(profiles, lengths, owners, block_mask):
    n = PLANES * ACROSS
    feats, size = profiles.shape[0], lengths.shape[0]
    half = size // 2
    lens = lengths.reshape(2, half // BLK, BLK)
    parts = [
        lax.dynamic_slice(
            profiles, (0, owners[t] * size), (feats, size), allow_negative_indices=False
        )
        for t in range(SECTIONS)
    ]
    out = pl.pallas_call(
        kernel,
        out_shape=jax.ShapeDtypeStruct((SECTIONS, size, half), jnp.bfloat16),
        in_specs=[
            pl.BlockSpec(memory_space=pl.ANY),
            pl.BlockSpec(memory_space=pl.ANY),
            pl.BlockSpec(memory_space=pl.ANY),
            pl.BlockSpec(memory_space=pl.ANY),
            pl.BlockSpec(memory_space=pltpu.SMEM),
            pl.BlockSpec(memory_space=pltpu.SMEM),
        ],
        out_specs=pl.BlockSpec(memory_space=pltpu.VMEM),
        scratch_shapes=[
            pltpu.VMEM(profiles.shape, jnp.bfloat16),
            pltpu.VMEM((feats, size), jnp.bfloat16),
            pltpu.VMEM((KM, size), jnp.bfloat16),
            pltpu.VMEM((KM, size), jnp.bfloat16),
            pltpu.VMEM((size, size), jnp.float32),
            pltpu.VMEM(lens.shape, jnp.int32),
            pltpu.VMEM((n,) + lens.shape[1:], jnp.int32),
            pltpu.SemaphoreType.DMA((6,)),
            pltpu.SemaphoreType.DMA,
            pltpu.SemaphoreType.DMA((n * 2 * 4,)),
            pltpu.SemaphoreType.DMA((n * 2,)),
            pltpu.SemaphoreType.DMA((n,)),
            pltpu.SemaphoreType.DMA((n * 2,)),
            pltpu.SemaphoreType.DMA((n,)),
            pltpu.SemaphoreType.DMA((n,)),
            pltpu.SemaphoreType.DMA((n,)),
        ],
        compiler_params=pltpu.CompilerParams(
            collective_id=0, has_side_effects=True, vmem_limit_bytes=48 * 1024 * 1024
        ),
        cost_estimate=pl.CostEstimate(
            flops=2 * KM * size * size, bytes_accessed=8 * 1024 * 1024, transcendentals=size * size
        ),
    )(profiles, *parts, lens, owners, block_mask)
    return out.transpose(1, 0, 2)


def solution(mesh):
    placed = (P(("seq", "kmer"), None), P("seq"), P(), P(None, "seq", None))
    n, cores = mesh.shape["seq"], mesh.shape["kmer"]
    fits = n == PLANES * ACROSS and cores == 2
    return jax.shard_map(
        fused if fits else shards,
        mesh=mesh, in_specs=placed, out_specs=P("seq", None, "kmer"), check_vma=False,
    )
```

```python
import functools

import jax
import jax.numpy as jnp
from jax import lax
from jax.experimental import pallas as pl
from jax.experimental.pallas import tpu as pltpu
from jax.sharding import PartitionSpec as P

KM = 2048
BLK = 128
SECTIONS = 2
MESH = pl.DeviceIdType.MESH


def broadcast(block, axis, source):
    block = jnp.where(lax.axis_index(axis) == source, block, jnp.zeros_like(block))
    return lax.psum(block, axis)


def shards(profiles, lengths, owners, block_mask):
    local = lax.all_to_all(profiles, "seq", split_axis=1, concat_axis=0, tiled=True)
    panel_rows = local.shape[1]
    half = panel_rows // 2
    part = lax.axis_index("kmer")
    row_len = lengths.astype(jnp.float32)
    scale = 256.0 / jnp.sqrt(jnp.float32(KM))
    contract = (((0,), (0,)), ((), ()))
    outs = []
    for section in range(SECTIONS):
        panel, panel_len = (
            broadcast(local, "seq", owners[section]),
            broadcast(lengths, "seq", owners[section]),
        )
        partial_value = lax.dot_general(local, panel, contract, preferred_element_type=jnp.float32)
        raw = lax.psum_scatter(partial_value, "kmer", scatter_dimension=1, tiled=True)
        col_len = lax.dynamic_slice_in_dim(panel_len.astype(jnp.float32), part * half, half, 0)
        mask_full = jnp.repeat(jnp.repeat(block_mask[section], BLK, axis=0), BLK, axis=1).astype(
            jnp.float32
        )
        mask = lax.dynamic_slice_in_dim(mask_full, part * half, half, 1)
        norm = scale * lax.rsqrt(row_len[:, None] * col_len[None, :])
        outs.append((raw * norm * mask).astype(jnp.bfloat16))
    return jnp.stack(outs, axis=1)


PLANES, ACROSS = 4, 4


def kernel(
    prof_hbm, first, second, lens_hbm, owners, mask, out, prof, ex, panel, local, acc, lens, lens_all,
    in_sem, ex_sem, p_send, p_recv, l_send, l_recv, f_send, len_send, len_recv,
):
    n = PLANES * ACROSS
    feats = prof.shape[0]
    size = local.shape[1]
    half = size // 2
    me, core = lax.axis_index("seq"), lax.axis_index("kmer")
    sib = 1 - core
    z, xy = lax.div(me, ACROSS), lax.rem(me, ACROSS)
    y, x = lax.div(xy, 2), lax.rem(xy, 2)
    xn = me + 1 - 2 * x
    yn = me + 2 * (1 - 2 * y)
    high = lax.div(z, 2)
    order = [z, z + 1 - 2 * lax.rem(z, 2), 2 - high, 3 - 3 * high]
    shift = [(p - z) * ACROSS for p in order]
    inner = jnp.logical_or(z == 1, z == 2)
    pair, middle = me + shift[1], me + ACROSS * (3 - 2 * z)

    def rows(place, c):
        return pl.ds(pl.multiple_of((place * 2 + c) * feats, feats), feats)

    def columns(start, length):
        return pl.ds(pl.multiple_of(start, length), length)

    def piece(place, c, slot, to):
        at = panel.at[rows(place, c)]
        i = place * 2 + c
        return pltpu.make_async_remote_copy(
            src_ref=at, dst_ref=at, send_sem=p_send.at[i * 4 + slot], recv_sem=p_recv.at[i],
            device_id=(to, core), device_id_type=MESH,
        )

    def block_to(to):
        return pltpu.make_async_remote_copy(
            src_ref=prof.at[:, columns(to * size, size)], dst_ref=local.at[rows(me, core)],
            send_sem=l_send.at[to], recv_sem=l_recv.at[me * 2 + core],
            device_id=(to, core), device_id_type=MESH,
        )

    def lens_to(to):
        return pltpu.make_async_remote_copy(
            src_ref=lens.at[core], dst_ref=lens_all.at[me],
            send_sem=len_send.at[to], recv_sem=len_recv.at[me],
            device_id=(to, core), device_id_type=MESH,
        )

    def hand_over(place, own=False):
        at = local.at[rows(place, core)]
        return pltpu.make_async_remote_copy(
            src_ref=prof.at[:, columns(me * size, size)] if own else at, dst_ref=at,
            send_sem=f_send.at[place], recv_sem=l_recv.at[place * 2 + core],
            device_id=(me, sib), device_id_type=MESH,
        )

    def local_arrived(place, c):
        at = local.at[rows(place, c)]
        pltpu.make_async_remote_copy(
            src_ref=at, dst_ref=at, send_sem=f_send.at[place], recv_sem=l_recv.at[place * 2 + c],
            device_id=(me, sib), device_id_type=MESH,
        ).wait_recv()

    load = pltpu.make_async_copy(prof_hbm, prof, in_sem.at[0])
    load.start()
    load_lens = pltpu.make_async_copy(lens_hbm, lens, in_sem.at[1])
    load_lens.start()

    own_half, other_half = columns(core * half, half), columns(sib * half, half)
    load_mine = []
    for t, part in enumerate((first, second)):
        spot = pl.ds(t * half, half)
        load_mine.append(pltpu.make_async_copy(
            part.at[:, own_half], panel.at[rows(me, core), spot], in_sem.at[2 + t]
        ))
        load_mine.append(pltpu.make_async_copy(
            part.at[:, other_half], ex.at[:, spot], in_sem.at[4 + t]
        ))
    for step in load_mine:
        step.start()

    barrier = pltpu.get_barrier_semaphore()

    @pl.loop(1, n)
    def _(i):
        pl.semaphore_signal(
            barrier, inc=1, device_id=(lax.rem(me + i, n), core), device_id_type=MESH
        )

    pl.semaphore_signal(barrier, inc=1, device_id=(me, sib), device_id_type=MESH)
    load.wait()
    load_lens.wait()
    for step in load_mine:
        step.wait()
    local[rows(me, core), :] = prof[:, columns(me * size, size)]
    lens_all[me] = lens[core]
    pl.semaphore_wait(barrier, n)

    exchange = pltpu.make_async_remote_copy(
        src_ref=ex, dst_ref=panel.at[rows(me, core)], send_sem=ex_sem,
        recv_sem=p_recv.at[me * 2 + core], device_id=(me, sib), device_id_type=MESH,
    )
    exchange.start()

    def spread(q, c):
        place = me + shift[q]
        if q == 0:
            piece(place, c, 0, pair).start()

            @pl.when(inner)
            def _():
                piece(place, c, 1, middle).start()
        else:
            piece(place, c, 0, pair).wait_recv()

            @pl.when(inner)
            def _():
                piece(place, c, 0, middle if q == 1 else pair).start()

        piece(place, c, 2, xn).start()
        piece(place, c, 3, yn).start()

    def cross(q):
        piece(xn + shift[q], 0, 3, yn).wait_recv()
        piece(xn + shift[q], 0, 3, yn).start()
        piece(yn + shift[q], 1, 2, xn).wait_recv()
        piece(yn + shift[q], 1, 2, xn).start()

    def pass_on(q):
        for j in range(ACROSS):
            if q == 0 and j == 0:
                continue
            place = order[q] * ACROSS + lax.rem(xy + j, ACROSS)
            local_arrived(place, core)
            hand_over(place).start()

    def multiply(q):
        for j in range(ACROSS):
            local_arrived(order[q] * ACROSS + lax.rem(xy + j, ACROSS), sib)
        piece(xn + shift[q], 1, 3, yn).wait_recv()
        piece(yn + shift[q], 0, 3, yn).wait_recv()
        diagonal = xn + yn - me + shift[q]
        for c in range(2):
            piece(diagonal, c, 0, yn).wait_recv()
        deep = ACROSS * 2 * feats
        span = pl.ds(pl.multiple_of(order[q] * deep, deep), deep)

        @pl.loop(0, size // 256)
        def _(i):
            at = pl.ds(pl.multiple_of(i * 256, 256), 256)
            value = lax.dot_general(
                local[span, at], panel[span, :], (((0,), (0,)), ((), ())),
                preferred_element_type=jnp.float32,
            )
            if q == 0:
                acc[at, :] = value
            else:
                acc[at, :] += value

    place = me
    piece(place, core, 0, pair).start()

    @pl.when(inner)
    def _():
        piece(place, core, 1, middle).start()

    piece(place, core, 2, xn).start()
    piece(place, core, 3, yn).start()
    hand_over(me, own=True).start()
    piece(place, sib, 0, pair).wait_recv()
    spread(0, sib)

    def send_blocks(planes):
        for j in range(ACROSS):
            for q in planes:
                if q == 0 and j == 0:
                    continue
                to = order[q] * ACROSS + lax.rem(xy + j, ACROSS)
                block_to(to).start()
                lens_to(to).start()

    send_blocks((3, 2))

    for q in range(1, PLANES):
        spread(q, 0)
        spread(q, 1)
        cross(q - 1)
        if q == 1:
            send_blocks((0, 1))
        if q >= 2:
            pass_on(q - 2)
        if q >= 3:
            multiply(q - 3)
    cross(3)
    pass_on(2)
    multiply(1)
    pass_on(3)
    multiply(2)

    @pl.loop(1, n)
    def _(i):
        other = lax.rem(me + i, n)
        pltpu.make_async_remote_copy(
            src_ref=lens.at[core], dst_ref=lens_all.at[other],
            send_sem=len_send.at[other], recv_sem=len_recv.at[other],
            device_id=(other, core), device_id_type=MESH,
        ).wait_recv()

    multiply(3)

    scale = 256.0 / jnp.sqrt(jnp.float32(KM))
    for t in range(SECTIONS):
        col_len = jnp.zeros(lens_all.shape[1:], jnp.int32)
        for i in range(n):
            off = owners[t] - i
            col_len += jnp.maximum(1 - off * off, 0) * lens_all[i]
        col_len = col_len.astype(jnp.float32)

        @pl.loop(0, 2)
        def _(h):
            for r in range(size // BLK // 2):
                i = h * (size // BLK // 2) + r
                row = lens[h, r:r + 1, :].astype(jnp.float32)
                row_len = jnp.broadcast_to(row, (BLK, BLK)).T
                at = pl.ds(pl.multiple_of(i * BLK, BLK), BLK)
                for j in range(half // BLK):
                    spot = slice(j * BLK, (j + 1) * BLK)
                    norm = scale * lax.rsqrt(row_len * col_len[j:j + 1, :])
                    scored = mask[t, i, core * (half // BLK) + j].astype(jnp.float32)
                    raw = acc[at, t * half + j * BLK:t * half + (j + 1) * BLK]
                    out[t, at, spot] = (raw * norm * scored).astype(out.dtype)

    exchange.wait_send()
    for c in range(2):
        piece(me, c, 0, pair).wait_send()
        piece(me, c, 2, xn).wait_send()
        piece(me, c, 3, yn).wait_send()
        for q in range(1, PLANES):
            piece(me + shift[q], c, 2, xn).wait_send()
            piece(me + shift[q], c, 3, yn).wait_send()

    @pl.when(inner)
    def _():
        for c in range(2):
            piece(me, c, 1, middle).wait_send()
            for q in range(1, PLANES):
                piece(me + shift[q], c, 0, pair).wait_send()

    for q in range(PLANES):
        piece(xn + shift[q], 0, 3, yn).wait_send()
        piece(yn + shift[q], 1, 2, xn).wait_send()
    hand_over(me, own=True).wait_send()

    @pl.loop(1, n)
    def _(i):
        other = lax.rem(me + i, n)
        block_to(other).wait_send()
        lens_to(other).wait_send()
        hand_over(other).wait_send()


def fused(profiles, lengths, owners, block_mask):
    n = PLANES * ACROSS
    feats, size = profiles.shape[0], lengths.shape[0]
    half = size // 2
    lens = lengths.reshape(2, half // BLK, BLK)
    parts = [
        lax.dynamic_slice(
            profiles, (0, owners[t] * size), (feats, size), allow_negative_indices=False
        )
        for t in range(SECTIONS)
    ]
    out = pl.pallas_call(
        kernel,
        out_shape=jax.ShapeDtypeStruct((SECTIONS, size, half), jnp.bfloat16),
        in_specs=[
            pl.BlockSpec(memory_space=pl.ANY),
            pl.BlockSpec(memory_space=pl.ANY),
            pl.BlockSpec(memory_space=pl.ANY),
            pl.BlockSpec(memory_space=pl.ANY),
            pl.BlockSpec(memory_space=pltpu.SMEM),
            pl.BlockSpec(memory_space=pltpu.SMEM),
        ],
        out_specs=pl.BlockSpec(memory_space=pltpu.VMEM),
        scratch_shapes=[
            pltpu.VMEM(profiles.shape, jnp.bfloat16),
            pltpu.VMEM((feats, size), jnp.bfloat16),
            pltpu.VMEM((KM, size), jnp.bfloat16),
            pltpu.VMEM((KM, size), jnp.bfloat16),
            pltpu.VMEM((size, size), jnp.float32),
            pltpu.VMEM(lens.shape, jnp.int32),
            pltpu.VMEM((n,) + lens.shape[1:], jnp.int32),
            pltpu.SemaphoreType.DMA((6,)),
            pltpu.SemaphoreType.DMA,
            pltpu.SemaphoreType.DMA((n * 2 * 4,)),
            pltpu.SemaphoreType.DMA((n * 2,)),
            pltpu.SemaphoreType.DMA((n,)),
            pltpu.SemaphoreType.DMA((n * 2,)),
            pltpu.SemaphoreType.DMA((n,)),
            pltpu.SemaphoreType.DMA((n,)),
            pltpu.SemaphoreType.DMA((n,)),
        ],
        compiler_params=pltpu.CompilerParams(
            collective_id=0, has_side_effects=True, vmem_limit_bytes=48 * 1024 * 1024
        ),
        cost_estimate=pl.CostEstimate(
            flops=2 * KM * size * size, bytes_accessed=8 * 1024 * 1024, transcendentals=size * size
        ),
    )(profiles, *parts, lens, owners, block_mask)
    return out.transpose(1, 0, 2)


def solution(mesh):
    placed = (P(("seq", "kmer"), None), P("seq"), P(), P(None, "seq", None))
    n, cores = mesh.shape["seq"], mesh.shape["kmer"]
    fits = n == PLANES * ACROSS and cores == 2
    return jax.shard_map(
        fused if fits else shards,
        mesh=mesh, in_specs=placed, out_specs=P("seq", None, "kmer"), check_vma=False,
    )
```
